32 devices in a mesh: expert: 4 (over y, core), shard: 8 (over z, x).
Axes of the slice: x: 2, y: 2, z: 4, core: 2. Of those that a mesh axis runs over, the one named last changes fastest.
Arguments:
- tokens: bfloat16 [16384, 1024], P(('expert', 'shard')), may hold values from -6 to 6
- cotangent: bfloat16 [16384, 1024], P(('expert', 'shard')), may hold values from -6 to 6
- routes: int32 [16384, 8], P(('expert', 'shard')), may hold values from 0 to 31, all different within a row; in each aligned block of 512 rows (0 to 511, 512 to 1023, ...) at most 256 rows name the same one
- segments: int32 [32, 512], P(('expert', 'shard')), may hold values from 0 to 7, never falling along the last dimension, each value on 1 to 256 neighbouring positions
- tile_counts: int32 [32, 32], P(('expert', 'shard')), may hold values from 1 to 2
- norm1_gain: bfloat16 [1024], P('shard'), may hold values from 0.5 to 1.5
- w_query: bfloat16 [1024, 1024], P('shard'), may hold values from -0.1875 to 0.1875
- w_key: bfloat16 [1024, 512], P('shard'), may hold values from -0.1875 to 0.1875
- w_value: bfloat16 [1024, 512], P('shard'), may hold values from -0.1875 to 0.1875
- w_out: bfloat16 [1024, 1024], P('shard'), may hold values from -0.75 to 0.75
- norm2_gain: bfloat16 [1024], P('shard'), may hold values from 0.5 to 1.5
- w_router: bfloat16 [1024, 32], P('shard'), may hold values from -0.1875 to 0.1875
- w_gate_up: bfloat16 [32, 1024, 1024], P('expert', 'shard'), may hold values from -0.1875 to 0.1875
- w_down: bfloat16 [32, 512, 1024], P('expert', 'shard'), may hold values from -0.75 to 0.75
Outputs:
- output: bfloat16 [16384, 1024], P(('expert', 'shard'))
- grad_tokens: float32 [16384, 1024], P(('expert', 'shard'))
- grad_norm1: float32 [1024], P('shard')
- grad_query: float32 [1024, 1024], P('shard')
- grad_key: float32 [1024, 512], P('shard')
- grad_value: float32 [1024, 512], P('shard')
- grad_out: float32 [1024, 1024], P('shard')
- grad_norm2: float32 [1024], P('shard')
- grad_router: float32 [1024, 32], P('shard')
- grad_gate_up: float32 [32, 1024, 1024], P('expert', 'shard')
- grad_down: float32 [32, 512, 1024], P('expert', 'shard')
The draws below stay inside these ranges and needn't reach their ends.
Inputs may be any that keep to these rules, and one draw needn't show every extreme that they name: `routes`: each token names 8 different experts; among the tokens of one sequence no expert is named more than 256 times. `segments`: never falling along a sequence; every document number of a sequence is used, each by at most half of 512 positions.
All inputs are finite; a program needn't handle non-finite values.
Results may differ from the reference program's by a relative error of at most 0.015.
Values may be sent and summed in bfloat16 or wider, within the bound.
A program may use at most 320 MiB of HBM per device.

```python
import math
import jax
import jax.numpy as jnp
import numpy as np
from jax import lax

D = 1024
H = 16
KVH = 8
HD = 64
FF = 512
EXPERTS = 32
TOP = 8
TOK_DEV = 512
TILE = 128
TILES = 2
DOCS = 8
SEQS = 32
TOKENS = 16384
CAP = 256


def plant(entries, own_key, smallest, largest):
    shape = entries.shape
    spot = [jax.random.randint(jax.random.fold_in(own_key, axis), (), 0, shape[axis]) for axis in range(len(shape))]
    entries = entries.at[tuple(spot)].set(smallest)
    longest = shape.index(max(shape))
    spot[longest] = (spot[longest] + 1) % shape[longest]
    return entries.at[tuple(spot)].set(largest)


def level_of(rng, extent, shards, smallest, largest):
    level, own = 1.0, jax.random.fold_in(rng, 6)
    for dim, shards_of in shards:
        heights = jnp.exp(jax.random.uniform(jax.random.fold_in(own, dim), (shards_of,), jnp.float32, smallest / len(shards), largest / len(shards)))
        level = level * jnp.repeat(heights, extent[dim] // shards_of).reshape([-1 if axis == dim else 1 for axis in range(len(extent))])
    return level


def profile(amount, total, limit, skew):
    weights = [(1 << 20) // math.isqrt(rank ** skew) + 1 for rank in range(2, amount + 1)]
    surplus, given = total - limit - (amount - 1), [1] * (amount - 1)
    while surplus > 0:
        movable = [i for i in range(amount - 1) if given[i] < limit]
        whole, left = sum([weights[i] for i in movable]), surplus
        for i in movable:
            extra = min(limit - given[i], max(1, left * weights[i] // whole), surplus)
            given[i] = given[i] + extra
            surplus = surplus - extra
    return np.array([limit] + given)


def ragged(key, amount, total, reach, lean):
    if amount == 2:
        one = jax.random.randint(key, (), max(1, total - reach), min(reach, total - 1) + 1)
        return jnp.stack([one, total - one])
    lengths = jnp.asarray(profile(amount, total, reach, lean), jnp.int32)
    pairs = (amount - 1) // 2
    giver, taker = lengths[1:1 + 2 * pairs:2], lengths[2:2 + 2 * pairs:2]
    slack = jnp.minimum(giver - 1, reach - taker)
    shifted = jax.random.randint(jax.random.fold_in(key, 1), (pairs,), 0, 1 << 20) % (slack + 1)
    lengths = lengths.at[1:1 + 2 * pairs:2].set(giver - shifted).at[2:2 + 2 * pairs:2].set(taker + shifted)
    return lengths[jax.random.permutation(jax.random.fold_in(key, 2), amount)]


def shared_out(own_key, own, number, rows, count, top, bound, skew):
    sequence = jax.random.permutation(own_key, count)
    heavy_load, common = shares(count, rows * top, bound, skew, True), shares(count, rows * top, bound, skew, False)
    places = jnp.arange(count)

    def named(lengths, offset_by):
        used = int((lengths > 0).sum())
        fixed = max(1, used // 4)
        shifted = fixed + (places - fixed + offset_by * (used - fixed)) % max(1, count - fixed)
        return jnp.zeros((count,), jnp.int32).at[sequence[jnp.where(places < fixed, places, shifted)]].set(jnp.asarray(lengths, jnp.int32))

    lengths = jnp.where(number % 4 == 0, named(heavy_load, number // 4), named(common, number - number // 4 - 1))
    mixed = jax.random.permutation(jax.random.fold_in(own, 3), count)
    giver, sink = mixed[0:count // 2 * 2:2], mixed[1:count // 2 * 2:2]
    room = jnp.minimum(lengths[giver] - 1, bound - lengths[sink]) // 2
    room = jnp.where((giver == sequence[0]) | (sink == sequence[0]) | (lengths[sink] == 0), 0, jnp.maximum(room, 0))
    shifted = jax.random.randint(jax.random.fold_in(own, 4), (count // 2,), 0, 1 << 20) % (room + 1)
    lengths = lengths.at[giver].add(-shifted).at[sink].add(shifted)
    items = jnp.searchsorted(jnp.cumsum(lengths), jnp.arange(rows * top), side="right").astype(jnp.int32)
    listing = items.reshape(top, rows).T
    listing = listing[jax.random.permutation(jax.random.fold_in(own, 1), rows)]
    offset_by = jax.random.randint(jax.random.fold_in(own, 2), (rows, 1), 0, top)
    return jnp.take_along_axis(listing, (jnp.arange(top)[None, :] + offset_by) % top, axis=1)


def shares(amount, total, most, slope, full):
    weights = [(1 << 20) // math.isqrt(standing ** slope) + 1 for standing in range(1, amount + 1)]
    largest = most if full else min(most, max(-(-total // amount), total * weights[0] // sum(weights)))
    least = 1 if total - largest >= amount - 1 else 0
    given, spare = [largest] + [least] * (amount - 1), total - largest - least * (amount - 1)
    while spare > 0:
        movable = [i for i in range(1, amount) if given[i] < largest] or [i for i in range(1, amount) if given[i] < most]
        mass, budget = sum([weights[i] for i in movable]), spare
        for i in movable:
            addition = min(most - given[i], max(1, budget * weights[i] // mass), spare)
            given[i] = given[i] + addition
            spare = spare - addition
    return np.array(given)


def normal_values(rng, extent, spread, limit, cuts=(), kind=jnp.bfloat16):
    loudness = level_of(rng, extent, cuts, -0.22, 0.18) if cuts else 1.0
    entries = jax.random.normal(rng, extent, jnp.float32) * spread * loudness
    return jnp.minimum(jnp.maximum(entries, -limit), limit).astype(kind)


def setup_inputs(seed: int = 0) -> dict:
    streams_of = jax.random.split(jax.random.key(seed), 15)
    tokens = normal_values(streams_of[0], (TOKENS, D), 1.0, 6.0, ((0, 32),))
    cotangent = normal_values(streams_of[1], (TOKENS, D), 1.0, 6.0, ((0, 32),))
    routes_keys = jax.random.split(jax.random.fold_in(streams_of[2], 1), TOKENS // TOK_DEV)
    routes_turns = jax.random.permutation(jax.random.fold_in(streams_of[2], 3), TOKENS // TOK_DEV)
    routes = jax.vmap(lambda own, number: shared_out(jax.random.fold_in(streams_of[2], 2), own, number, TOK_DEV, EXPERTS, TOP, CAP, 2))(routes_keys, routes_turns).reshape((TOKENS, TOP))
    segments = jax.vmap(lambda own: jnp.searchsorted(jnp.cumsum(ragged(own, DOCS, TOK_DEV, TOK_DEV // 2, 2)), jnp.arange(TOK_DEV), side="right"))(jax.random.split(streams_of[3], SEQS)).reshape((SEQS, TOK_DEV)).astype(jnp.int32)
    tile_counts = plant(jax.random.randint(streams_of[4], (SEQS, EXPERTS), 1, TILES + 1), jax.random.fold_in(streams_of[4], 1), 1, TILES).astype(jnp.int32)
    norm1_gain = jnp.clip(1.0 + 0.1 * jax.random.normal(streams_of[5], (D,), jnp.float32), 0.5, 1.5).astype(jnp.bfloat16)
    w_query = normal_values(streams_of[6], (D, H * HD), D ** -0.5, 0.1875, ((0, 8),))
    w_key = normal_values(streams_of[7], (D, KVH * HD), D ** -0.5, 0.1875, ((0, 8),))
    w_value = normal_values(streams_of[8], (D, KVH * HD), D ** -0.5, 0.1875, ((0, 8),))
    w_out = normal_values(streams_of[9], (H * HD, D), (D // 16) ** -0.5, 0.75, ((0, 8),))
    norm2_gain = jnp.clip(1.0 + 0.1 * jax.random.normal(streams_of[10], (D,), jnp.float32), 0.5, 1.5).astype(jnp.bfloat16)
    w_router = normal_values(streams_of[11], (D, EXPERTS), D ** -0.5, 0.1875, ((0, 8),))
    w_gate_up = normal_values(streams_of[12], (EXPERTS, D, 2 * FF), D ** -0.5, 0.1875, ((0, 4), (1, 8)))
    w_down = normal_values(streams_of[13], (EXPERTS, FF, D), (FF // 8) ** -0.5, 0.75, ((0, 4), (1, 8)))
    return {"tokens": tokens, "cotangent": cotangent, "routes": routes, "segments": segments, "tile_counts": tile_counts, "norm1_gain": norm1_gain, "w_query": w_query, "w_key": w_key, "w_value": w_value, "w_out": w_out, "norm2_gain": norm2_gain, "w_router": w_router, "w_gate_up": w_gate_up, "w_down": w_down}


EPSILON = 1e-06
ROTARY_BASE = 10000.0
MASKED = -1e+30

@jax.custom_vjp
def low(v):
    return lax.optimization_barrier(v.astype(jnp.bfloat16)).astype(jnp.float32)

@jax.custom_vjp
def low_back(v):
    return v

def low_keep(v):
    return (low(v), None)

def low_pass(kept, grad):
    return (grad,)

def back_keep(v):
    return (v, None)

def back_low(kept, grad):
    return (low(grad),)
low.defvjp(low_keep, low_pass)
low_back.defvjp(back_keep, back_low)

def rotary_tables(length, head_size):
    halfway = head_size // 2
    exponent = jnp.arange(halfway, dtype=jnp.float32) * (2.0 / head_size)
    angles = jnp.arange(length, dtype=jnp.float32)[:, None] * (ROTARY_BASE ** (-exponent))[None, :]
    cosine = jnp.concatenate([jnp.cos(angles), jnp.cos(angles)], -1)
    sine = jnp.concatenate([jnp.sin(angles), jnp.sin(angles)], -1)
    return (cosine, sine)

def rotate(values, cosine, sine):
    halfway = values.shape[-1] // 2
    turned = jnp.concatenate([-values[..., halfway:], values[..., :halfway]], -1)
    return values * cosine[:, None, :] + turned * sine[:, None, :]

def normed(values, gain):
    return values * lax.rsqrt(lax.optimization_barrier(jnp.mean(values * values, -1, keepdims=True)) + EPSILON) * gain

def one_sequence(inputs, route, document, counts, params):
    gain_first, query_weight, key_weight, value_weight, output_weight, gain_second, router_weight, joined_weight, down_weight = params
    highest = lax.Precision.HIGHEST
    length = inputs.shape[0]
    normed_low = low(normed(inputs, gain_first))
    cosine, sine = rotary_tables(length, HD)
    query = low(rotate(low_back(jnp.dot(normed_low, query_weight, precision=highest)).reshape(length, H, HD), cosine, sine))
    keys = low(rotate(low_back(jnp.dot(normed_low, key_weight, precision=highest)).reshape(length, KVH, HD), cosine, sine))
    values = low(low_back(jnp.dot(normed_low, value_weight, precision=highest))).reshape(length, KVH, HD)
    query = query.reshape(length, KVH, H // KVH, HD)
    scores = low_back(jnp.einsum('qkgd,tkd->kgqt', query, keys, precision=highest) * HD ** (-0.5))
    places = jnp.arange(length)
    allowed = (document[:, None] == document[None, :]) & (places[:, None] >= places[None, :])
    scores = jnp.where(allowed[None, None], scores, MASKED)
    expo = jnp.exp(scores - lax.optimization_barrier(jnp.max(scores, -1, keepdims=True)))
    probs = low(expo / lax.optimization_barrier(jnp.sum(expo, -1, keepdims=True)))
    attended = low(low_back(jnp.einsum('kgqt,tkd->qkgd', probs, values, precision=highest))).reshape(length, H * HD)
    residual = inputs + low_back(jnp.dot(attended, output_weight, precision=highest))
    mixed = low(normed(residual, gain_second))
    logits = jnp.dot(mixed, router_weight, precision=highest)
    onehot = (route[:, :, None] == jnp.arange(EXPERTS, dtype=jnp.int32)[None, None, :]).astype(jnp.int32)
    chosen = lax.optimization_barrier(jnp.sum(logits[:, None, :] * onehot.astype(jnp.float32), -1))
    chosen_exp = jnp.exp(chosen - lax.optimization_barrier(jnp.max(chosen, -1, keepdims=True)))
    gating = chosen_exp / lax.optimization_barrier(jnp.sum(chosen_exp, -1, keepdims=True))
    flat_hot = onehot.reshape(length * TOP, EXPERTS)
    ranking = lax.optimization_barrier(jnp.sum((jnp.cumsum(flat_hot, 0).astype(jnp.int32) - flat_hot) * flat_hot, -1)).astype(jnp.int32)
    limits = (TILE * lax.optimization_barrier(jnp.sum(flat_hot * counts[None, :], -1))).astype(jnp.int32)
    kept = ranking < limits
    placed = (route.reshape(-1) * CAP + ranking).astype(jnp.int32)
    target = jnp.where(kept, placed, EXPERTS * CAP).astype(jnp.int32)
    pickup = jnp.minimum(placed, EXPERTS * CAP - 1).astype(jnp.int32)
    owners = (jnp.arange(length * TOP) // TOP).astype(jnp.int32)
    buffer = jnp.zeros((EXPERTS * CAP, inputs.shape[1]), jnp.float32).at[target].set(mixed[owners], mode='drop')
    buffer = low_back(buffer).reshape(EXPERTS, CAP, inputs.shape[1])
    joined = low_back(jnp.einsum('ecm,emf->ecf', buffer, joined_weight, precision=highest))
    gate_pre = joined[..., :FF]
    up_pre = joined[..., FF:]
    hidden = low(gate_pre * jax.nn.sigmoid(gate_pre) * up_pre)
    expert_out = low(low_back(jnp.einsum('ecf,efm->ecm', hidden, down_weight, precision=highest)))
    expert_out = expert_out.reshape(EXPERTS * CAP, inputs.shape[1])
    picked = (expert_out[pickup] * kept.astype(jnp.float32)[:, None]).reshape(length, TOP, inputs.shape[1])
    return residual + lax.optimization_barrier(jnp.sum(gating[:, :, None] * picked, 1))

def reference(tokens, cotangent, routes, segments, tile_counts, norm1_gain, w_query, w_key, w_value, w_out, norm2_gain, w_router, w_gate_up, w_down):
    params = tuple((weight.astype(jnp.float32) for weight in (norm1_gain, w_query, w_key, w_value, w_out, norm2_gain, w_router, w_gate_up, w_down)))
    group = min(SEQS, max(1, 2048 // TOK_DEV))
    turns = SEQS // group
    inputs = tokens.astype(jnp.float32).reshape(turns, group, TOK_DEV, D)
    upstream = cotangent.astype(jnp.float32).reshape(turns, group, TOK_DEV, D)
    route_all = routes.reshape(turns, group, TOK_DEV, TOP)
    document_all = segments.reshape(turns, group, TOK_DEV)
    count_all = tile_counts.reshape(turns, group, EXPERTS)

    def one_group(totals, items):
        group_in, group_up, group_route, group_doc, group_count = items

        def run(weights, values):
            return jax.vmap(lambda a, b, c, d: one_sequence(a, b, c, d, weights))(values, group_route, group_doc, group_count)
        result, pullback = jax.vjp(run, params, group_in)
        weight_grads, input_grads = pullback(group_up)
        totals = jax.tree.map(jnp.add, totals, weight_grads)
        return (totals, (result.astype(jnp.bfloat16), input_grads))
    zeros = jax.tree.map(jnp.zeros_like, params)
    totals, (outputs, input_grads) = lax.scan(one_group, zeros, (inputs, upstream, route_all, document_all, count_all))
    return (outputs.reshape(TOKENS, D), input_grads.reshape(TOKENS, D), totals[0], totals[1], totals[2], totals[3], totals[4], totals[5], totals[6], totals[7], totals[8])
```

```python
import functools

import jax
import jax.numpy as jnp
from jax import lax
from jax.experimental import pallas as pl
from jax.experimental.pallas import tpu as pltpu
from jax.sharding import PartitionSpec as P

D = 1024
H = 16
KVH = 8
HD = 64
FF = 512
EXPERTS = 32
TOP = 8
TILE = 128
CAP = 256
PLANE = 8
QKV = H * HD + 2 * KVH * HD
PACKED = QKV + D + 128

EPSILON = 1e-06
ROTARY_BASE = 10000.0
MASKED = -1e30

BF = jnp.bfloat16
F32 = jnp.float32
HBM = pl.BlockSpec(memory_space=pltpu.HBM)
VMEM = pl.BlockSpec(memory_space=pltpu.VMEM)
DMA = pltpu.SemaphoreType.DMA
LIMIT = 62 * 1024 * 1024 - 512 * 1024


def dot(a, b):
    return jnp.dot(a, b, preferred_element_type=F32)


def dot_nt(a, b):
    return lax.dot_general(a, b, (((1,), (1,)), ((), ())), preferred_element_type=F32)


def dot_tn(a, b):
    return lax.dot_general(a, b, (((0,), (0,)), ((), ())), preferred_element_type=F32)


def flip(value, bit):
    return value + bit * (1 - 2 * ((value // bit) % 2))


class Sizes:
    def __init__(self, mesh):
        self.holders = mesh.shape["expert"]
        self.shards = mesh.shape["shard"]
        self.f = PLANE // self.holders
        self.n = self.shards // self.f
        self.experts = EXPERTS // PLANE
        self.rows = D // self.shards
        self.rows_down = FF // self.shards
        self.parts = min(self.holders, self.rows // 16)
        self.part = self.rows // self.parts
        self.piece = self.f * (self.rows + self.rows_down)


class Here:
    def __init__(self, t):
        self.t = t
        self.e = lax.axis_index("expert")
        self.idx = lax.axis_index("shard")
        self.r = self.idx // t.f
        self.sub = self.idx % t.f
        self.g = self.e * t.f + self.sub
        self.core = t.f
        self.b1, self.b2 = [b for b in (1, 2, 4) if b != t.f]
        self.pc = flip(self.g, self.core)
        self.p1 = flip(self.g, self.b1)
        self.p2 = flip(self.g, self.b2)
        self.pd = flip(self.p1, self.b2)
        self.mate = flip(self.g, 1)

    def dev(self, g, r=None):
        r = self.r if r is None else r
        return {"expert": g // self.t.f, "shard": r * self.t.f + g % self.t.f}

    def member(self, m):
        g = self.g
        for b in (1, 2, 4):
            if m & b:
                g = flip(g, b)
        return g

    def barrier(self, plane=True, line=True):
        t, r = self.t, self.r
        sem = pltpu.get_barrier_semaphore()
        count = 0
        if plane:
            for m in range(1, PLANE):
                signal(sem, self.dev(self.member(m)))
            count = PLANE - 1
        if line:
            first, last = r == 0, r == t.n - 1
            pl.when(jnp.logical_not(first))(lambda: signal(sem, self.dev(self.g, r - 1)))
            pl.when(jnp.logical_not(last))(lambda: signal(sem, self.dev(self.g, r + 1)))
            pl.when(first | last)(lambda: pl.semaphore_wait(sem, count + 1))
            pl.when(jnp.logical_not(first | last))(lambda: pl.semaphore_wait(sem, count + 2))
        else:
            pl.semaphore_wait(sem, count)


def signal(sem, device):
    pl.semaphore_signal(sem, inc=1, device_id=device, device_id_type=pl.DeviceIdType.MESH)


def remote(src, dst, send, recv, device):
    return pltpu.make_async_remote_copy(
        src_ref=src,
        dst_ref=dst,
        send_sem=send,
        recv_sem=recv,
        device_id=device,
        device_id_type=pl.DeviceIdType.MESH,
    )


class LineGather:
    def __init__(self, here, blk, ss, rs):
        self.h, self.blk, self.ss, self.rs = here, blk, ss, rs

    def copy(self, p, way, r):
        return remote(self.blk(p), self.blk(p), self.ss(way, p), self.rs(p), self.h.dev(self.h.g, r))

    def step(self, s):
        h, n = self.h, self.h.t.n
        r = h.r

        def right():
            c = self.copy(r - s, 0, r + 1)
            if s:
                c.wait_recv()
            c.start()

        def left():
            c = self.copy(r + s, 1, r - 1)
            if s:
                c.wait_recv()
            c.start()

        pl.when((r >= s) & (r < n - 1))(right)
        pl.when((r + s <= n - 1) & (r > 0))(left)

    def fin(self):
        h, n = self.h, self.h.t.n
        r = h.r
        for p in range(n):
            c = self.copy(p, 0, r)
            pl.when(((r > p) & (r == n - 1)) | ((r < p) & (r == 0)))(c.wait_recv)

    def drain(self):
        h, n = self.h, self.h.t.n
        r = h.r
        for s in range(n - 1):
            pl.when((r >= s) & (r < n - 1))(lambda: self.copy(r - s, 0, r + 1).wait_send())
            pl.when((r + s <= n - 1) & (r > 0))(lambda: self.copy(r + s, 1, r - 1).wait_send())


class PlaneGather:
    COUNT = 9

    def __init__(self, here, blk, half, ss, rs, own=None, ok=None):
        h = here
        own = blk(h.g) if own is None else own
        self.ok = ok
        self.ss, self.rs, self.h = ss, rs, h
        self.out = [
            (own, blk(h.g), h.pc, h.g),
            (own, blk(h.g), h.p1, h.g),
            (own, blk(h.g), h.p2, h.g),
            (half(h.p1, 0), half(h.p1, 0), h.p2, h.p1),
            (half(h.p2, 1), half(h.p2, 1), h.p1, h.p2),
            (blk(h.p1), blk(h.p1), h.pc, h.p1),
            (blk(h.p2), blk(h.p2), h.pc, h.p2),
            (half(h.pd, 0), half(h.pd, 0), h.pc, h.pd),
            (half(h.pd, 1), half(h.pd, 1), h.pc, h.pd),
        ]
        c1, c2 = flip(h.pc, h.b1), flip(h.pc, h.b2)
        cd = flip(c1, h.b2)
        self.arrive = [
            (blk(h.pc), h.pc),
            (blk(h.p1), h.p1),
            (blk(h.p2), h.p2),
            (half(h.pd, 0), h.pd),
            (half(h.pd, 1), h.pd),
            (blk(c1), c1),
            (blk(c2), c2),
            (half(cd, 0), cd),
            (half(cd, 1), cd),
        ]

    def guard(self, origin, fn):
        if self.ok is None:
            fn()
        else:
            pl.when(self.ok(origin))(fn)

    def make(self, i):
        src, dst, peer, origin = self.out[i]
        return remote(src, dst, self.ss(i), self.rs(i), self.h.dev(peer)), origin

    def send(self, *which):
        for i in which:
            c, origin = self.make(i)
            self.guard(origin, c.start)

    def wait(self, *which):
        for i in which:
            dst, origin = self.arrive[i]
            c = remote(dst, dst, self.ss(i), self.rs(i), self.h.dev(self.h.pc))
            self.guard(origin, c.wait_recv)

    def start(self):
        self.send(1, 2, 0)

    def second(self):
        self.wait(1)
        self.send(3, 5)
        self.wait(2)
        self.send(4, 6)

    def third(self):
        self.wait(3)
        self.send(7)
        self.wait(4)
        self.send(8)

    def fin(self):
        self.wait(0, 5, 6, 7, 8)

    def drain(self):
        for i in range(self.COUNT):
            c, origin = self.make(i)
            self.guard(origin, c.wait_send)


class Mates:
    def __init__(self, here, pairs, ss, rs):
        self.h, self.pairs, self.ss, self.rs = here, pairs, ss, rs

    def copies(self, el):
        return [
            (remote(src, there, self.ss(el, k), self.rs(el, k), self.h.dev(self.h.mate)),
             remote(mine, mine, self.ss(el, k), self.rs(el, k), self.h.dev(self.h.mate)))
            for k, (src, there, mine) in enumerate(self.pairs(el))
        ]

    def start(self, el):
        if self.h.t.f > 1:
            for c, _ in self.copies(el):
                c.start()

    def wait(self, el):
        if self.h.t.f > 1:
            for _, c in self.copies(el):
                c.wait_recv()

    def drain(self, el):
        if self.h.t.f > 1:
            for c, _ in self.copies(el):
                c.wait_send()


def rope(block, cosine, sine_a, sine_b):
    return block * cosine + pltpu.roll(block, 96, 1) * sine_a + pltpu.roll(block, 32, 1) * sine_b


def first_kernel(
    t,
    x_ref, routes_ref, doc_row_ref, doc_col_ref, counts_ref, cos_ref, sin_a_ref, sin_b_ref,
    g_in, packed_in, gu_in, down_in,
    w_out, ga_out, h2_out, info_out, packed_out, res_ref, att_ref, q_ref, k_ref, v_ref, p_out, gate_ref,
    aw, bias, p_stage, h2_stage, info_stage, loc, one_s, one_r, aw_ls, aw_lr, aw_ps, aw_pr,
    mate_s, mate_r, w_ls, w_lr, g_ps, g_pr, h_ps, h_pr, i_s, i_r, p_sem,
):
    h = Here(t)
    n, r, sub, E = t.n, h.r, h.sub, t.experts
    q = h.e % t.parts
    h.barrier()

    def awb(g, *rest):
        return aw.at[:, g % t.f, (g // t.f) % t.parts]

    ok = None if t.parts == t.holders else (lambda g: g // t.f < t.parts)
    half_rows = PACKED // 2 // 128 * 128

    def aw_half(g, k):
        lo, size = ((0, half_rows), (half_rows, PACKED - half_rows))[k]
        return aw.at[:, g % t.f, (g // t.f) % t.parts, :, pl.ds(lo, size)]

    gu_rows = lambda s: pl.ds(s * t.rows, t.rows)
    down_rows = lambda s: pl.ds(t.f * t.rows + s * t.rows_down, t.rows_down)

    own = [
        pltpu.make_async_copy(packed_in.at[pl.ds(q * t.part, t.part)], aw.at[r, sub, q], loc.at[0]),
        pltpu.make_async_copy(gu_in.at[pl.ds(sub * E, E)], w_out.at[:, r, gu_rows(sub)], loc.at[1]),
        pltpu.make_async_copy(down_in.at[pl.ds(sub * E, E)], w_out.at[:, r, down_rows(sub)], loc.at[2]),
        pltpu.make_async_copy(g_in, ga_out.at[h.g], loc.at[3]),
    ]
    for c in own:
        c.start()
    other = t.f - 1 - sub
    mates = Mates(
        h,
        lambda el: [
            (gu_in.at[other * E + el], w_out.at[el, r, gu_rows(sub)], w_out.at[el, r, gu_rows(other)]),
            (down_in.at[other * E + el], w_out.at[el, r, down_rows(sub)], w_out.at[el, r, down_rows(other)]),
        ],
        lambda el, k: mate_s.at[el, k],
        lambda el, k: mate_r.at[el, k],
    )
    mates.start(0)
    mates.start(1)
    line_a = LineGather(h, lambda p: aw.at[p, sub, q], lambda way, p: aw_ls.at[way, p], lambda p: aw_lr.at[p])
    lines = [
        LineGather(
            h,
            lambda p, el=el: w_out.at[el, p],
            lambda way, p, el=el: w_ls.at[el, way, p],
            lambda p, el=el: w_lr.at[el, p],
        )
        for el in range(E)
    ]
    plane_a = PlaneGather(h, awb, aw_half, lambda i: aw_ps.at[i], lambda i: aw_pr.at[i], ok=ok)
    rows_half = lambda ref: (lambda g, k: ref.at[g, pl.ds(k * 256, 256)])
    plane_g = PlaneGather(
        h, lambda g: ga_out.at[g], rows_half(ga_out), lambda i: g_ps.at[i], lambda i: g_pr.at[i], own=g_in
    )
    plane_h = PlaneGather(
        h, lambda g: h2_out.at[g], rows_half(h2_out), lambda i: h_ps.at[i], lambda i: h_pr.at[i], own=h2_stage
    )
    own[0].wait()
    for s in range(n - 1):
        line_a.step(s)
    line_a.fin()
    plane_a.start()
    own[1].wait()
    own[2].wait()
    for el in (0, 1):
        mates.wait(el)
        lines[el].step(0)
    mates.start(2)
    mates.start(3)

    length = x_ref.shape[0]
    same = doc_col_ref[...] == doc_row_ref[...]
    before = lax.broadcasted_iota(jnp.int32, (length, length), 0) >= lax.broadcasted_iota(
        jnp.int32, (length, length), 1
    )
    bias[...] = jnp.where(same & before, 0.0, MASKED)
    expert_rows = lax.broadcasted_iota(jnp.int32, (EXPERTS, length), 0)
    routed = jnp.zeros((EXPERTS, length), F32)
    for k in range(TOP):
        routed = routed + jnp.where(expert_rows == routes_ref[k : k + 1, :], 1.0, 0.0)
    earlier = jnp.where(
        lax.broadcasted_iota(jnp.int32, (length, length), 0) < lax.broadcasted_iota(jnp.int32, (length, length), 1),
        1.0,
        0.0,
    ).astype(BF)
    rank = dot(routed.astype(BF), earlier)
    kept = (routed > 0.5) & (rank < counts_ref[...] * float(TILE))
    slot = jnp.where(kept, rank, -1.0)

    plane_a.second()
    plane_a.third()
    plane_a.fin()
    for s in range(1, n - 1):
        lines[0].step(s)
    plane_g.start()
    own[3].wait()
    keep = pltpu.make_async_copy(aw, packed_out, loc.at[4])
    keep.start()

    tail = aw[:, :, :, :, QKV + D : PACKED].reshape(D, PACKED - QKV - D).astype(F32).T
    gain_one, gain_two = tail[EXPERTS : EXPERTS + 1, :], tail[EXPERTS + 1 : EXPERTS + 2, :]
    x = x_ref[...].astype(F32)
    scale = lax.rsqrt(jnp.mean(x * x, -1, keepdims=True) + EPSILON)
    a1 = (x * scale * gain_one).astype(BF)
    cosine, sine_a, sine_b = cos_ref[...], sin_a_ref[...], sin_b_ref[...]
    weight = lambda lo, hi: aw[:, :, :, :, lo:hi].reshape(D, hi - lo)
    for c in range(2):
        block = dot(a1, weight(c * 512, c * 512 + 512))
        for b in range(4):
            q_ref[4 * c + b] = rope(block[:, b * 128 : b * 128 + 128], cosine, sine_a, sine_b).astype(BF)
    block = dot(a1, weight(H * HD, H * HD + KVH * HD))
    for b in range(4):
        turned = rope(block[:, b * 128 : b * 128 + 128], cosine, sine_a, sine_b).astype(BF)
        k_ref[2 * b] = turned[:, :HD]
        k_ref[2 * b + 1] = turned[:, HD:]
    block = dot(a1, weight(H * HD + KVH * HD, QKV)).astype(BF)
    for b in range(KVH):
        v_ref[b] = block[:, b * HD : b * HD + HD]
    for s in range(1, n - 1):
        lines[1].step(s)
    for el in (2, 3):
        mates.wait(el)
        lines[el].step(0)

    def heads(b, carry):
        pair = q_ref[b]
        stacked = jnp.concatenate([pair[:, :HD], pair[:, HD:]], 0)
        scores = dot_nt(stacked, k_ref[b]) * HD ** (-0.5)
        scores = scores.reshape(2, length, length) + bias[...][None]
        top = jnp.max(scores, -1, keepdims=True)
        raised = jnp.exp(scores - top)
        total = jnp.sum(raised, -1, keepdims=True)
        probs = (raised / total).astype(BF).reshape(2 * length, length)

        @pl.when(b >= 2)
        def _():
            pltpu.make_async_copy(p_stage.at[b % 2], p_out.at[b], p_sem.at[b % 2]).wait()

        p_stage[b % 2] = probs
        pltpu.make_async_copy(p_stage.at[b % 2], p_out.at[b], p_sem.at[b % 2]).start()
        mixed = dot(probs, v_ref[b]).astype(BF)
        att_ref[:, pl.ds(pl.multiple_of(b * 128, 128), 128)] = jnp.concatenate(
            [mixed[:length], mixed[length:]], 1
        )
        return carry

    lax.fori_loop(0, KVH, heads, 0)
    for b in range(2):
        pltpu.make_async_copy(p_stage.at[b], p_out.at[b], p_sem.at[b]).wait()
    plane_g.second()

    residual = x + dot(att_ref[...], weight(QKV, QKV + D))
    res_ref[...] = residual
    scale_two = lax.rsqrt(jnp.mean(residual * residual, -1, keepdims=True) + EPSILON)
    h2 = (residual * scale_two * gain_two).astype(BF)
    h2_stage[...] = h2
    plane_h.start()
    logits = dot(h2, weight(QKV + D, PACKED)).T[:EXPERTS, :]
    highest = jnp.max(jnp.where(routed > 0.5, logits, MASKED), 0, keepdims=True)
    raised = jnp.where(routed > 0.5, jnp.exp(jnp.minimum(logits - highest, 0.0)), 0.0)
    gate = raised / jnp.sum(raised, 0, keepdims=True)
    gate_ref[...] = gate
    for g in range(PLANE):
        info_stage[g, 0:E, :] = slot[g * E : g * E + E, :]
        info_stage[g, E : 2 * E, :] = gate[g * E : g * E + E, :]
    infos = []
    for m in range(1, PLANE):
        g = h.member(m)
        infos.append(
            (remote(info_stage.at[g], info_out.at[h.g], i_s.at[m], i_r.at[m], h.dev(g)),
             remote(info_out.at[g], info_out.at[g], i_s.at[m], i_r.at[m], h.dev(g)))
        )
        infos[-1][0].start()
    mine = [
        pltpu.make_async_copy(info_stage.at[h.g], info_out.at[h.g], loc.at[5]),
        pltpu.make_async_copy(h2_stage, h2_out.at[h.g], loc.at[6]),
    ]
    for c in mine:
        c.start()
    plane_g.third()
    plane_h.second()
    plane_h.third()
    for el in (2, 3):
        for s in range(1, n - 1):
            lines[el].step(s)
    plane_g.fin()
    plane_h.fin()
    for c, landed in infos:
        landed.wait_recv()
    for line in lines:
        line.fin()
    for c in mine:
        c.wait()
    keep.wait()
    line_a.drain()
    plane_a.drain()
    plane_g.drain()
    plane_h.drain()
    for line in lines:
        line.drain()
    for el in range(E):
        mates.drain(el)
    for c, _ in infos:
        c.wait_send()


def first(t, x, routes_t, doc_row, doc_col, counts, cosine, sine_a, sine_b, g, packed, gu, down):
    length = x.shape[0]
    E, n = t.experts, t.n
    shape = jax.ShapeDtypeStruct
    aw_shape = (n, t.f, t.parts, t.part, PACKED)
    return pl.pallas_call(
        functools.partial(first_kernel, t),
        out_shape=(
            shape((E, n, t.piece, D), BF),
            shape((PLANE, length, D), BF),
            shape((PLANE, length, D), BF),
            shape((PLANE, 2 * E, length), F32),
            shape(aw_shape, BF),
            shape((length, D), F32),
            shape((length, H * HD), BF),
            shape((KVH, length, 128), BF),
            shape((KVH, length, HD), BF),
            shape((KVH, length, HD), BF),
            shape((KVH, 2 * length, length), BF),
            shape((EXPERTS, length), F32),
        ),
        in_specs=[VMEM] * 8 + [HBM] * 4,
        out_specs=(HBM, HBM, HBM, HBM, HBM, VMEM, VMEM, VMEM, VMEM, VMEM, HBM, VMEM),
        scratch_shapes=[
            pltpu.VMEM(aw_shape, BF),
            pltpu.VMEM((length, length), F32),
            pltpu.VMEM((2, 2 * length, length), BF),
            pltpu.VMEM((length, D), BF),
            pltpu.VMEM((PLANE, 2 * E, length), F32),
            DMA((8,)),
            DMA((1,)),
            DMA((1,)),
            DMA((2, n)),
            DMA((n,)),
            DMA((9,)),
            DMA((9,)),
            DMA((E, 2)),
            DMA((E, 2)),
            DMA((E, 2, n)),
            DMA((E, n)),
            DMA((9,)),
            DMA((9,)),
            DMA((9,)),
            DMA((9,)),
            DMA((8,)),
            DMA((8,)),
            DMA((2,)),
        ],
        compiler_params=pltpu.CompilerParams(
            collective_id=1, has_side_effects=True, vmem_limit_bytes=LIMIT
        ),
        cost_estimate=pl.CostEstimate(flops=12 * 10**9, bytes_accessed=60 * 2**20, transcendentals=5 * 10**6),
        name="attention_forward",
    )(x, routes_t, doc_row, doc_col, counts, cosine, sine_a, sine_b, g, packed, gu, down)


class LineReduce:
    def __init__(self, here, own, buf, ss, rs):
        self.h, self.own, self.buf, self.ss, self.rs = here, own, buf, ss, rs

    def slot(self, way, d, r):
        return d - r if way == 0 else self.h.t.n - r + d

    def serve(self, way, d):
        h, n = self.h, self.h.t.n
        r = h.r
        to = r + 1 if way == 0 else r - 1
        target = self.buf(self.slot(way, d, to))
        began = (r == 0) if way == 0 else (r == n - 1)

        def begin():
            remote(self.own(d), target, self.ss(way, d), self.rs(way, d), h.dev(h.g, to)).start()

        def go_on():
            here = self.buf(self.slot(way, d, r))
            c = remote(here, target, self.ss(way, d), self.rs(way, d), h.dev(h.g, to))
            remote(here, here, self.ss(way, d), self.rs(way, d), h.dev(h.g, to)).wait_recv()
            here[...] = (here[...].astype(F32) + self.own(d)[...].astype(F32)).astype(BF)
            c.start()

        pl.when(began)(begin)
        pl.when(jnp.logical_not(began))(go_on)

    def turn(self, k):
        h, n = self.h, self.h.t.n
        r = h.r
        j = k - r
        d = n - 1 - j
        pl.when((j >= 0) & (d > r))(lambda: self.serve(0, d))
        j2 = k - (n - 1 - r)
        pl.when((j2 >= 0) & (j2 < r))(lambda: self.serve(1, j2))

    def fin(self):
        h, n = self.h, self.h.t.n
        r = h.r
        mine = self.own(r)

        def add(way):
            here = self.buf(self.slot(way, r, r))
            remote(here, here, self.ss(way, r), self.rs(way, r), h.dev(h.g, r)).wait_recv()
            mine[...] = (here[...].astype(F32) + mine[...].astype(F32)).astype(BF)

        pl.when(r > 0)(lambda: add(0))
        pl.when(r < n - 1)(lambda: add(1))

    def drain(self):
        h, n = self.h, self.h.t.n
        r = h.r
        for d in range(n):
            c = [
                remote(self.own(d), self.buf(0), self.ss(way, d), self.rs(way, d), h.dev(h.g, r))
                for way in (0, 1)
            ]
            pl.when(d > r)(c[0].wait_send)
            pl.when(d < r)(c[1].wait_send)


def second_kernel(
    t,
    info_ref, w_in, h2_in, g_in,
    y_out, row_out, dgate_out, gu_out, down_out,
    w, xs, dj, hid, dy, h2_buf, g_buf, y_stage, row_stage, grads, landed, dg,
    w_sem, in_sem, out_sem, ls, lr, mate_s, mate_r, loc, d_s, d_r,
):
    h = Here(t)
    n, r, sub, E = t.n, h.r, h.sub, t.experts
    h.barrier()
    length = h2_in.shape[1]
    gu_piece, down_piece = t.f * t.rows, t.f * t.rows_down
    dg[...] = jnp.zeros_like(dg)

    def load(step, k):
        s = step % PLANE
        return (
            pltpu.make_async_copy(h2_in.at[s], h2_buf.at[k], in_sem.at[0, k]),
            pltpu.make_async_copy(g_in.at[s], g_buf.at[k], in_sem.at[1, k]),
        )

    def stores(el, s, k):
        return (
            pltpu.make_async_copy(y_stage.at[k], y_out.at[s, el], out_sem.at[0, k]),
            pltpu.make_async_copy(row_stage.at[k], row_out.at[s, el], out_sem.at[1, k]),
        )

    def reducer(el):
        return LineReduce(
            h,
            lambda p: grads.at[el, p],
            lambda k: landed.at[el, k],
            lambda way, p: ls.at[el, way, p],
            lambda way, p: lr.at[el, way, p],
        )

    turns = 2 * (n - 1)

    def serve(tau):
        for el in range(E):
            k = tau - 2 * (el + 1)
            pl.when((k >= 0) & (k < turns))(lambda k=k, el=el: reducer(el).turn(k))

    for c in load(0, 0):
        c.start()
    slots = lax.broadcasted_iota(jnp.int32, (CAP, length), 0).astype(F32)

    def expert(el, carry):
        fetch = pltpu.make_async_copy(w_in.at[el], w, w_sem.at[0])
        fetch.start()
        fetch.wait()

        def sequence(s, carry):
            step = el * PLANE + s
            k = s % 2

            @pl.when(step + 1 < E * PLANE)
            def _():
                for c in load(step + 1, 1 - k):
                    c.start()

            for c in load(step, k):
                c.wait()
            slot_row = info_ref[s, pl.ds(el, 1), :]
            gate_row = info_ref[s, pl.ds(E + el, 1), :]
            hit = slots == slot_row
            pick = jnp.where(hit, 1.0, 0.0).astype(BF)
            gate = jnp.sum(jnp.where(hit, gate_row, 0.0), 1, keepdims=True)
            rows = pl.ds(pl.multiple_of(s * CAP, CAP), CAP)
            x = dot(pick, h2_buf[k]).astype(BF)
            xs[rows, :] = x
            g = dot(pick, g_buf[k])
            d_out = (gate * g).astype(BF)
            dy[rows, :] = d_out
            w_gu = w[:, 0:gu_piece, :].reshape(D, 2 * FF)
            w_down = w[:, gu_piece : gu_piece + down_piece, :].reshape(FF, D)
            joined = dot(x, w_gu)
            gate_pre, up_pre = joined[:, :FF], joined[:, FF:]
            sigmoid = jax.nn.sigmoid(gate_pre)
            active = gate_pre * sigmoid
            hidden = (active * up_pre).astype(BF)
            hid[rows, :] = hidden
            y = dot(hidden, w_down)
            d_gate = jnp.sum(g * y, 1, keepdims=True)
            dg[s, pl.ds(el, 1), :] = jnp.sum(jnp.where(hit, d_gate, 0.0), 0, keepdims=True)

            @pl.when(step >= 2)
            def _():
                for c in stores(el, s, k):
                    c.wait()

            y_stage[k] = (gate * y).astype(BF)
            d_hidden = dot_nt(d_out, w_down)
            d_joined = jnp.concatenate(
                [
                    d_hidden * up_pre * sigmoid * (1.0 + gate_pre * (1.0 - sigmoid)),
                    d_hidden * active,
                ],
                1,
            ).astype(BF)
            dj[rows, :] = d_joined
            row_stage[k] = dot_nt(d_joined, w_gu).astype(BF)
            for c in stores(el, s, k):
                c.start()
            for turn in range(2):
                pl.when(s == 4 * turn + 2)(lambda: serve(2 * el + turn))
            return carry

        lax.fori_loop(0, PLANE, sequence, 0)

        def tile(i, carry):
            cols = pl.ds(pl.multiple_of(i * 256, 256), 256)
            part = dot_tn(xs[:, cols], dj[...]).astype(BF)
            many = 256 * n // D
            if many <= 1:
                grads[el, i // (D // 256 // n), pl.ds(0, 256), :] = part
            else:
                grads[el, pl.ds(i * many, many), 0:gu_piece, :] = part.reshape(many, gu_piece, 2 * FF)
            return carry

        lax.fori_loop(0, D // 256, tile, 0)

        def tile_down(i, carry):
            cols = pl.ds(pl.multiple_of(i * 256, 256), 256)
            part = dot_tn(hid[:, cols], dy[...]).astype(BF)
            many = 256 * n // FF
            grads[el, pl.ds(i * many, many), gu_piece : gu_piece + down_piece, :] = part.reshape(
                many, down_piece, D
            )
            return carry

        lax.fori_loop(0, FF // 256, tile_down, 0)
        return carry

    lax.fori_loop(0, E, expert, 0)
    for k in range(2):
        for c in stores(E - 1, PLANE - 2 + k, k):
            c.wait()
    sends = []
    for m in range(1, PLANE):
        g = h.member(m)
        sends.append(
            (remote(dg.at[g], dgate_out.at[h.g], d_s.at[m], d_r.at[m], h.dev(g)),
             remote(dgate_out.at[g], dgate_out.at[g], d_s.at[m], d_r.at[m], h.dev(g)))
        )
        sends[-1][0].start()
    mine = [pltpu.make_async_copy(dg.at[h.g], dgate_out.at[h.g], loc.at[0])]
    mine[0].start()

    other = t.f - 1 - sub
    parts = lambda s: (pl.ds(s * t.rows, t.rows), pl.ds(gu_piece + s * t.rows_down, t.rows_down))
    mates = Mates(
        h,
        lambda el: [
            (grads.at[el, r, parts(other)[0]], gu_out.at[sub * E + el], gu_out.at[other * E + el]),
            (grads.at[el, r, parts(other)[1]], down_out.at[sub * E + el], down_out.at[other * E + el]),
        ],
        lambda el, k: mate_s.at[el, k],
        lambda el, k: mate_r.at[el, k],
    )
    for tau in range(2 * E, 2 * E + turns):
        serve(tau)
        for el in range(E):
            if tau == 2 * (el + 1) + turns - 1 or (tau == 2 * E and 2 * (el + 1) + turns - 1 < 2 * E):
                reducer(el).fin()
                mates.start(el)
                for k, (src, dst) in enumerate(
                    (
                        (grads.at[el, r, parts(sub)[0]], gu_out.at[sub * E + el]),
                        (grads.at[el, r, parts(sub)[1]], down_out.at[sub * E + el]),
                    )
                ):
                    mine.append(pltpu.make_async_copy(src, dst, loc.at[1 + 2 * el + k]))
                    mine[-1].start()
    for el in range(E):
        mates.wait(el)
    for _, c in sends:
        c.wait_recv()
    for c in mine:
        c.wait()
    for el in range(E):
        reducer(el).drain()
        mates.drain(el)
    for c, _ in sends:
        c.wait_send()


def second(t, info, w, h2, g):
    length = h2.shape[1]
    E, n = t.experts, t.n
    shape = jax.ShapeDtypeStruct
    return pl.pallas_call(
        functools.partial(second_kernel, t),
        out_shape=(
            shape((PLANE, E, CAP, D), BF),
            shape((PLANE, E, CAP, D), BF),
            shape((PLANE, 2 * E, length), F32),
            shape((t.f * E, t.rows, 2 * FF), BF),
            shape((t.f * E, t.rows_down, D), BF),
        ),
        in_specs=[VMEM] + [HBM] * 3,
        out_specs=(HBM,) * 5,
        scratch_shapes=[
            pltpu.VMEM((n, t.piece, D), BF),
            pltpu.VMEM((PLANE * CAP, D), BF),
            pltpu.VMEM((PLANE * CAP, 2 * FF), BF),
            pltpu.VMEM((PLANE * CAP, FF), BF),
            pltpu.VMEM((PLANE * CAP, D), BF),
            pltpu.VMEM((2, length, D), BF),
            pltpu.VMEM((2, length, D), BF),
            pltpu.VMEM((2, CAP, D), BF),
            pltpu.VMEM((2, CAP, D), BF),
            pltpu.VMEM((E, n, t.piece, D), BF),
            pltpu.VMEM((E, n + 1, t.piece, D), BF),
            pltpu.VMEM((PLANE, 2 * E, length), F32),
            DMA((1,)),
            DMA((2, 2)),
            DMA((2, 2)),
            DMA((E, 2, n)),
            DMA((E, 2, n)),
            DMA((E, 2)),
            DMA((E, 2)),
            DMA((1 + 2 * E,)),
            DMA((PLANE,)),
            DMA((PLANE,)),
        ],
        compiler_params=pltpu.CompilerParams(
            collective_id=2, has_side_effects=True, vmem_limit_bytes=LIMIT
        ),
        cost_estimate=pl.CostEstimate(flops=110 * 10**9, bytes_accessed=200 * 2**20, transcendentals=5 * 10**6),
        name="experts",
    )(info, w, h2, g)


def third_kernel(
    t,
    info_ref, y_in, row_in,
    y_out, row_out,
    ybuf, rbuf, stage, from_core, own, near1, near2, last, in_sem, cs, cr, ns, nr,
):
    h = Here(t)
    h.barrier(line=False)
    E = t.experts
    length = stage.shape[2]
    half = length // 2
    order = [(core, b1, b2) for core in (1, 0) for b1, b2 in ((1, 1), (1, 0), (0, 1), (0, 0))]

    def target(i):
        g = h.g
        for on, bit in zip(order[i], (h.core, h.b1, h.b2)):
            if on:
                g = flip(g, bit)
        return g

    def load(i):
        g = target(i)
        k = i % 2
        return (
            pltpu.make_async_copy(row_in.at[g], rbuf.at[k], in_sem.at[0, k]),
            pltpu.make_async_copy(y_in.at[g], ybuf.at[k], in_sem.at[1, k]),
        )

    lanes = lax.broadcasted_iota(jnp.int32, (length, CAP), 1).astype(F32)

    def near(tensor, way, k, src, peer):
        buf = (near1, near2)[way]
        return remote(src, buf.at[tensor, k], ns.at[tensor, way, k], nr.at[tensor, way, k], h.dev(peer))

    def arrived(tensor, way, k):
        buf = (near1, near2)[way].at[tensor, k]
        remote(buf, buf, ns.at[tensor, way, k], nr.at[tensor, way, k], h.dev(h.pc)).wait_recv()
        return (near1, near2)[way][tensor, k].astype(F32)

    for c in load(0):
        c.start()
    lo, hi = pl.ds(0, half), pl.ds(half, half)
    sent = []
    for i in range(8):
        if i < 7:
            for c in load(i + 1):
                c.start()
        columns = info_ref[target(i)].T
        spread = jnp.concatenate(
            [jnp.where(lanes == columns[:, el : el + 1], 1.0, 0.0).astype(BF) for el in range(E)], 1
        )
        for tensor in range(2):
            load(i)[tensor].wait()
            rows = (rbuf, ybuf)[tensor][i % 2].reshape(E * CAP, D)
            block = dot(spread, rows)
            j = i % 4
            if i < 4:
                stage[tensor, j] = block.astype(BF)
                c = remote(
                    stage.at[tensor, j], from_core.at[tensor, j], cs.at[tensor, j], cr.at[tensor, j], h.dev(h.pc)
                )
                c.start()
                sent.append(c)
                continue
            remote(
                from_core.at[tensor, j], from_core.at[tensor, j], cs.at[tensor, j], cr.at[tensor, j], h.dev(h.pc)
            ).wait_recv()
            own[tensor, j] = (block + from_core[tensor, j].astype(F32)).astype(BF)
            whole = own.at[tensor, j]
            if j == 0:
                new = [near(tensor, 0, 0, whole.at[lo], h.p1), near(tensor, 1, 0, whole.at[hi], h.p2)]
            elif j == 1:
                new = [near(tensor, 0, 1, whole.at[lo], h.p1)]
            elif j == 2:
                new = [near(tensor, 1, 1, whole.at[hi], h.p2)]
            else:
                new = []
            for c in new:
                c.start()
            sent += new
    for tensor in range(2):
        own[tensor, 1, hi] = (own[tensor, 1, hi].astype(F32) + arrived(tensor, 1, 0)).astype(BF)
        own[tensor, 2, lo] = (own[tensor, 2, lo].astype(F32) + arrived(tensor, 0, 0)).astype(BF)
        new = [
            near(tensor, 0, 2, own.at[tensor, 1, hi], h.p1),
            near(tensor, 1, 2, own.at[tensor, 2, lo], h.p2),
        ]
        for c in new:
            c.start()
        sent += new
    for tensor, out in ((0, row_out), (1, y_out)):
        out[lo, :] = own[tensor, 3, lo].astype(F32) + arrived(tensor, 0, 1) + arrived(tensor, 1, 2)
        out[hi, :] = own[tensor, 3, hi].astype(F32) + arrived(tensor, 1, 1) + arrived(tensor, 0, 2)
    for c in sent:
        c.wait_send()


def third(t, info, y, rows):
    length = info.shape[2]
    E = t.experts
    shape = jax.ShapeDtypeStruct
    return pl.pallas_call(
        functools.partial(third_kernel, t),
        out_shape=(shape((length, D), F32), shape((length, D), F32)),
        in_specs=[VMEM, HBM, HBM],
        out_specs=(VMEM, VMEM),
        scratch_shapes=[
            pltpu.VMEM((2, E, CAP, D), BF),
            pltpu.VMEM((2, E, CAP, D), BF),
            pltpu.VMEM((2, 4, length, D), BF),
            pltpu.VMEM((2, 4, length, D), BF),
            pltpu.VMEM((2, 4, length, D), BF),
            pltpu.VMEM((2, 3, length // 2, D), BF),
            pltpu.VMEM((2, 3, length // 2, D), BF),
            pltpu.VMEM((8, 128), F32),
            DMA((2, 2)),
            DMA((2, 4)),
            DMA((2, 4)),
            DMA((2, 2, 3)),
            DMA((2, 2, 3)),
        ],
        compiler_params=pltpu.CompilerParams(
            collective_id=3, has_side_effects=True, vmem_limit_bytes=LIMIT
        ),
        cost_estimate=pl.CostEstimate(flops=17 * 10**9, bytes_accessed=40 * 2**20, transcendentals=0),
        name="combine",
    )(info, y, rows)


def rotary_tables(length):
    halfway = HD // 2
    exponent = jnp.arange(halfway, dtype=F32) * (2.0 / HD)
    angles = jnp.arange(length, dtype=F32)[:, None] * (ROTARY_BASE ** (-exponent))[None, :]
    cosine, sine, none = jnp.cos(angles), jnp.sin(angles), jnp.zeros_like(angles)
    return (
        jnp.concatenate([cosine] * 4, -1),
        jnp.concatenate([-sine, none, -sine, none], -1),
        jnp.concatenate([none, sine, none, sine], -1),
    )


def rotate(values, cosine, sine):
    halfway = values.shape[-1] // 2
    turned = jnp.concatenate([-values[..., halfway:], values[..., :halfway]], -1)
    return values * cosine[:, None, :] + turned * sine[:, None, :]


def local(
    t,
    tokens, cotangent, routes, segments, tile_counts, norm1_gain, w_query, w_key, w_value, w_out,
    norm2_gain, w_router, w_gate_up, w_down,
):
    length = tokens.shape[0]
    groups = H // KVH
    highest = lax.Precision.HIGHEST
    rows = t.rows
    packed = jnp.concatenate(
        [
            w_query, w_key, w_value, w_out, w_router, norm1_gain[:, None], norm2_gain[:, None],
            jnp.zeros((rows, PACKED - QKV - D - EXPERTS - 2), BF),
        ],
        1,
    )
    cosine, sine_a, sine_b = rotary_tables(length)
    counts = jnp.broadcast_to(tile_counts.reshape(EXPERTS, 1).astype(F32), (EXPERTS, length))
    (
        w_all, g_all, h2_all, info, packed_all, residual, attended_low, q_all, k_all, v_all, p_all, gating
    ) = first(
        t, tokens, routes.T, segments, segments.reshape(length, 1), counts, cosine, sine_a, sine_b,
        cotangent, packed, w_gate_up, w_down,
    )
    y_slots, row_slots, dgate_all, joined_share, down_share = second(t, info, w_all, h2_all, g_all)
    y_sum, row_sum = third(t, info, y_slots, row_slots)

    full = packed_all.reshape(D, PACKED)
    query_weight = full[:, : H * HD]
    key_weight = full[:, H * HD : H * HD + KVH * HD]
    value_weight = full[:, H * HD + KVH * HD : QKV]
    output_weight = full[:, QKV : QKV + D]
    router_weight = full[:, QKV + D : QKV + D + EXPERTS]
    gain_one = full[:, QKV + D + EXPERTS].astype(F32)
    gain_two = full[:, QKV + D + EXPERTS + 1].astype(F32)
    inputs = tokens.astype(F32)
    upstream = cotangent.astype(F32)
    scale_first = lax.rsqrt(jnp.mean(inputs * inputs, -1, keepdims=True) + EPSILON)
    normed_low = (inputs * scale_first * gain_one).astype(BF)
    scale_second = lax.rsqrt(jnp.mean(residual * residual, -1, keepdims=True) + EPSILON)
    mixed_low = (residual * scale_second * gain_two).astype(BF)
    cosine, sine = cosine[:, :HD], (sine_b - sine_a)[:, :HD]
    query_low = q_all.reshape(KVH, length, groups, HD).transpose(1, 0, 2, 3)
    key_low = k_all.transpose(1, 0, 2)
    value_low = v_all.transpose(1, 0, 2)
    output = (residual + y_sum).astype(BF)
    gating_grad = dgate_all[:, : t.experts].reshape(EXPERTS, length)
    chosen_grad = gating * (gating_grad - jnp.sum(gating * gating_grad, 0, keepdims=True))
    logits_grad = chosen_grad.T
    router_grad = jnp.dot(mixed_low.astype(F32).T, logits_grad, precision=highest)
    mixed_grad = jnp.dot(logits_grad, router_weight.astype(F32).T, precision=highest) + row_sum
    gained_two = gain_two * mixed_grad
    gain_two_grad = jnp.sum(mixed_grad * residual * scale_second, 0)
    residual_grad = (
        upstream
        + scale_second * gained_two
        - residual * scale_second**3 * jnp.mean(gained_two * residual, -1, keepdims=True)
    )
    branch_low = residual_grad.astype(BF)
    output_weight_grad = jnp.einsum("sn,sm->nm", attended_low, branch_low, preferred_element_type=F32)
    attended_grad = jnp.einsum("sm,nm->sn", branch_low, output_weight, preferred_element_type=F32)
    attended_grad = attended_grad.astype(BF).reshape(length, KVH, groups, HD)
    probs_again = p_all.reshape(KVH, groups, length, length)
    probs = probs_again.astype(F32)
    value_grad = jnp.einsum("kgqt,qkgd->tkd", probs_again, attended_grad, preferred_element_type=F32)
    probs_grad = jnp.einsum("qkgd,tkd->kgqt", attended_grad, value_low, preferred_element_type=F32)
    scores_grad = (probs * (probs_grad - jnp.sum(probs * probs_grad, -1, keepdims=True))).astype(BF)
    query_grad = jnp.einsum("kgqt,tkd->qkgd", scores_grad, key_low, preferred_element_type=F32).reshape(
        length, H, HD
    ) * HD ** (-0.5)
    key_grad = jnp.einsum("kgqt,qkgd->tkd", scores_grad, query_low, preferred_element_type=F32) * HD ** (-0.5)
    query_back = rotate(query_grad, cosine, -sine).astype(BF).reshape(length, H * HD)
    key_back = rotate(key_grad, cosine, -sine).astype(BF).reshape(length, KVH * HD)
    value_back = value_grad.astype(BF).reshape(length, KVH * HD)
    query_weight_grad = jnp.einsum("sm,sn->mn", normed_low, query_back, preferred_element_type=F32)
    key_weight_grad = jnp.einsum("sm,sn->mn", normed_low, key_back, preferred_element_type=F32)
    value_weight_grad = jnp.einsum("sm,sn->mn", normed_low, value_back, preferred_element_type=F32)
    normed_grad = jnp.einsum("sn,mn->sm", query_back, query_weight, preferred_element_type=F32)
    normed_grad = normed_grad + jnp.einsum("sn,mn->sm", key_back, key_weight, preferred_element_type=F32)
    normed_grad = normed_grad + jnp.einsum("sn,mn->sm", value_back, value_weight, preferred_element_type=F32)
    gained_one = gain_one * normed_grad
    gain_one_grad = jnp.sum(normed_grad * inputs * scale_first, 0)
    token_grad = (
        residual_grad
        + scale_first * gained_one
        - inputs * scale_first**3 * jnp.mean(gained_one * inputs, -1, keepdims=True)
    )
    summed = lax.psum(
        (
            gain_one_grad, query_weight_grad, key_weight_grad, value_weight_grad, output_weight_grad,
            gain_two_grad, router_grad,
        ),
        ("expert", "shard"),
    )
    member = lax.axis_index("shard")
    shares = tuple(
        lax.dynamic_slice_in_dim(total, member * (total.shape[0] // t.shards), total.shape[0] // t.shards, 0)
        for total in summed
    )
    return (output, token_grad) + shares + (joined_share.astype(F32), down_share.astype(F32))


def solution(mesh):
    both, rows, held = P(("expert", "shard"), None), P("shard", None), P("expert", "shard", None)
    in_specs = (both,) * 5 + (P("shard"), rows, rows, rows, rows, P("shard"), rows, held, held)
    out_specs = (both, both, P("shard"), rows, rows, rows, rows, P("shard"), rows, held, held)
    return jax.shard_map(
        functools.partial(local, Sizes(mesh)), mesh=mesh, in_specs=in_specs, out_specs=out_specs, check_vma=False
    )
```
